128 devices in a mesh: pool: 2 (over y_lo), ctx: 4 (over z), mp: 16 (over y_hi, x, core).
Axes of the slice: x: 4, y: 4 (y_hi: 2, y_lo: 2; y = y_hi * 2 + y_lo), z: 4, core: 2. Of those that a mesh axis runs over, the one named last changes fastest.
Arguments:
- tokens: bfloat16 [2, 2048, 4096], P('pool', 'ctx', 'mp'), may hold values from -2.5 to 2.5
- norm_gain: float32 [4096], replicated, may hold values from 0.5 to 1.5
- cross_gain: float32 [4096], replicated, may hold values from 0.1 to 1.9
- w_query: bfloat16 [4096, 4096], P(None, 'mp'), may hold values from -8 to 8
- w_key: bfloat16 [4096, 4096], P(None, 'mp'), may hold values from -0.09375 to 0.09375
- w_value: bfloat16 [4096, 4096], P(None, 'mp'), may hold values from -0.09375 to 0.09375
- w_out: bfloat16 [4096, 4096], P('mp'), may hold values from -0.125 to 0.125
- w_cross_query: bfloat16 [4096, 4096], P(None, 'mp'), may hold values from -8 to 8
- w_cross_kv: bfloat16 [2, 896, 4096], P(None, None, 'mp'), may hold values from -0.1875 to 0.1875
- w_cross_out: bfloat16 [4096, 4096], P('mp'), may hold values from -0.125 to 0.125
- encoded: bfloat16 [512, 128, 896], P(('pool', 'ctx'), 'mp'), may hold values from -6 to 6
- owners: int32 [2, 32, 2], replicated, may hold values from 0 to 7, all different within a row; in each aligned block of 8 rows (0 to 7, 8 to 15, ..., all dimensions but the last counted through in order) at most 4 rows name the same one
- slots: int32 [2, 32, 2], replicated, may hold values from 0 to 63
Outputs:
- layer_out: bfloat16 [2, 2048, 4096], P('pool', 'ctx', 'mp')
The draws below stay inside these ranges and needn't reach their ends.
Inputs may be any that keep to these rules, and one draw needn't show every extreme that they name: The 2 neighbours of a span have different owners; among the spans of one index of pool and ctx (aligned blocks of 8 spans, sequence by sequence) no owner is named more than 4 times.
All inputs are finite; a program needn't handle non-finite values.
Results may differ from the reference program's by a relative error of at most 0.035.
Values may be sent and summed in bfloat16 or wider, within the bound.
No kernel may reach another device: no remote copies, remote signals or barrier semaphores. Data moves between devices by JAX's collectives and lax.ppermute only.
A program may use at most 128 MiB of HBM per device.

```python
import math
import jax
import jax.numpy as jnp
import numpy as np
from jax import lax

D = 4096
HEADS = 32
HEAD = 128
ENC_W = 896
SPAN = 64
NB_TOK = 128
NB_PER = 2
TOK_DEV = 512
ENC_DEV = 64
SEQS = 2
LEN = 2048
SPANS = 32
SP_DEV = 8
ENC_ROWS = 512
CAP = 4
N_POOL = 2
N_CTX = 4
N_MP = 16


def draw_w_query(key, part):
    key = jax.random.fold_in(key, 11)
    base = jax.random.normal(key, (D, D), jnp.float32)
    factor = jnp.exp(jax.random.uniform(jax.random.fold_in(key, 5), (HEADS,), jnp.float32, 0.0, math.log(2.0)))
    return (base * D ** (-0.5) * jnp.repeat(factor, HEAD)[None, :]).astype(jnp.bfloat16)


def draw_w_cross_query(key, part):
    key = jax.random.fold_in(key, 23)
    base = jax.random.normal(key, (D, D), jnp.float32)
    factor = jnp.exp(jax.random.uniform(jax.random.fold_in(key, 9), (HEADS,), jnp.float32, 0.0, math.log(3.0)))
    return (base * D ** (-0.5) * jnp.repeat(factor, HEAD)[None, :]).astype(jnp.bfloat16)


def touch_ends(drawn, key, smallest, top_value):
    dims = drawn.shape
    index_at = [jax.random.randint(jax.random.fold_in(key, axis), (), 0, dims[axis]) for axis in range(len(dims))]
    drawn = drawn.at[tuple(index_at)].set(smallest)
    longest = dims.index(max(dims))
    index_at[longest] = (index_at[longest] + 1) % dims[longest]
    return drawn.at[tuple(index_at)].set(top_value)


def strengthened(result, stream_key, source, target, blocks, factor):
    owner, partner = [(jnp.arange(result.shape[axis_at]) // (result.shape[axis_at] // blocks)).reshape([-1 if axis == axis_at else 1 for axis in range(result.ndim)]) for axis_at in (source, target)]
    chosen = jax.random.permutation(stream_key, blocks)[partner]
    strong = (owner == chosen) | (owner == (partner + blocks // 2) % blocks)
    return jnp.where(strong, factor * result, result)


def block_scale(rng, extent, split, least, largest):
    factor_of = 1.0
    for axis_at, parts in split:
        draws = jax.random.uniform(jax.random.fold_in(jax.random.fold_in(rng, 6), axis_at), (parts,), jnp.float32, least / len(split), largest / len(split))
        factor_of = factor_of * jnp.repeat(jnp.exp(draws), extent[axis_at] // parts).reshape((-1,) + (1,) * (len(extent) - 1 - axis_at))
    return factor_of


def deal_out(stream_key, own, number, rows, count, top, reach, lean):
    order = jax.random.permutation(stream_key, count)
    heavy_load, usual = portions_of(count, rows * top, reach, lean, True), portions_of(count, rows * top, reach, lean, False)
    places = jnp.arange(count)

    def named(lengths, turn):
        used = int((lengths > 0).sum())
        fixed = max(1, used // 4)
        passed = fixed + (places - fixed + turn * (used - fixed)) % max(1, count - fixed)
        return jnp.zeros((count,), jnp.int32).at[order[jnp.where(places < fixed, places, passed)]].set(jnp.asarray(lengths, jnp.int32))

    lengths = jnp.where(number % 4 == 0, named(heavy_load, number // 4), named(usual, number - number // 4 - 1))
    mixed = jax.random.permutation(jax.random.fold_in(own, 3), count)
    donor, taker = mixed[0:count // 2 * 2:2], mixed[1:count // 2 * 2:2]
    room = jnp.minimum(lengths[donor] - 1, reach - lengths[taker]) // 2
    room = jnp.where((donor == order[0]) | (taker == order[0]) | (lengths[taker] == 0), 0, jnp.maximum(room, 0))
    passed = jax.random.randint(jax.random.fold_in(own, 4), (count // 2,), 0, 1 << 20) % (room + 1)
    lengths = lengths.at[donor].add(-passed).at[taker].add(passed)
    members = jnp.searchsorted(jnp.cumsum(lengths), jnp.arange(rows * top), side="right").astype(jnp.int32)
    table = members.reshape(top, rows).T
    table = table[jax.random.permutation(jax.random.fold_in(own, 1), rows)]
    turn = jax.random.randint(jax.random.fold_in(own, 2), (rows, 1), 0, top)
    return jnp.take_along_axis(table, (jnp.arange(top)[None, :] + turn) % top, axis=1)


def portions_of(count, total, limit, skew, full):
    loads = [(1 << 20) // math.isqrt(rank ** skew) + 1 for rank in range(1, count + 1)]
    largest = limit if full else min(limit, max(-(-total // count), total * loads[0] // sum(loads)))
    least = 1 if total - largest >= count - 1 else 0
    counts, spare = [largest] + [least] * (count - 1), total - largest - least * (count - 1)
    while spare > 0:
        candidates = [i for i in range(1, count) if counts[i] < largest] or [i for i in range(1, count) if counts[i] < limit]
        mass, left = sum([loads[i] for i in candidates]), spare
        for i in candidates:
            addition = min(limit - counts[i], max(1, left * loads[i] // mass), spare)
            counts[i] = counts[i] + addition
            spare = spare - addition
    return np.array(counts)


def noise(key, dims, scale, most, split=(), kind=jnp.bfloat16):
    gain = block_scale(key, dims, split, -0.22, 0.18) if split else 1.0
    drawn = jax.random.normal(key, dims, jnp.float32) * scale * gain
    return jnp.minimum(jnp.maximum(drawn, -most), most).astype(kind)


def heavy_noise(stream_key, shape, spread, bound, pieces, heavy, held_as=jnp.bfloat16):
    drawn = spread * jax.random.normal(stream_key, shape, jnp.float32)
    if pieces:
        drawn = drawn * block_scale(stream_key, shape, pieces, -0.22, 0.18)
    return jnp.clip(strengthened(drawn, jax.random.fold_in(stream_key, 3), *heavy), -bound, bound).astype(held_as)


def setup_inputs(seed: int = 0) -> dict:
    arg_keys = jax.random.split(jax.random.key(seed), 14)
    tokens = noise(arg_keys[0], (SEQS, LEN, D), 0.4, 2.5, ((0, 2), (1, 4), (2, 16)))
    norm_gain = jnp.clip(1.0 + 0.1 * jax.random.normal(arg_keys[1], (D,), jnp.float32), 0.5, 1.5)
    cross_gain = jnp.clip(1.0 + 0.18 * jax.random.normal(arg_keys[2], (D,), jnp.float32), 0.1, 1.9)
    w_query = draw_w_query(jax.random.fold_in(arg_keys[13], 71), 0)
    w_key = noise(arg_keys[4], (D, D), D ** -0.5, 0.09375, ((1, 16),))
    w_value = noise(arg_keys[5], (D, D), D ** -0.5, 0.09375, ((1, 16),))
    w_out = heavy_noise(arg_keys[6], (D, D), D ** -0.5, 0.125, ((0, 16),), (0, 1, 16, 2.0))
    w_cross_query = draw_w_cross_query(jax.random.fold_in(arg_keys[13], 71), 0)
    w_cross_kv = noise(arg_keys[8], (2, ENC_W, D), ENC_W ** -0.5, 0.1875, ((2, 16),))
    w_cross_out = heavy_noise(arg_keys[9], (D, D), D ** -0.5, 0.125, ((0, 16),), (0, 1, 16, 2.0))
    encoded = noise(arg_keys[10], (ENC_ROWS, NB_TOK, ENC_W), 1.0, 6.0, ((0, 8), (1, 16)))
    owners_keys = jax.random.split(jax.random.fold_in(arg_keys[11], 1), SEQS * SPANS // SP_DEV)
    owners_turns = jax.random.permutation(jax.random.fold_in(arg_keys[11], 3), SEQS * SPANS // SP_DEV)
    owners = jax.vmap(lambda own, number: deal_out(jax.random.fold_in(arg_keys[11], 2), own, number, SP_DEV, N_POOL * N_CTX, NB_PER, CAP, 2))(owners_keys, owners_turns).reshape((SEQS, SPANS, NB_PER))
    slots = touch_ends(jax.random.randint(arg_keys[12], (SEQS, SPANS, NB_PER), 0, ENC_DEV), jax.random.fold_in(arg_keys[12], 1), 0, ENC_DEV - 1).astype(jnp.int32)
    return {"tokens": tokens, "norm_gain": norm_gain, "cross_gain": cross_gain, "w_query": w_query, "w_key": w_key, "w_value": w_value, "w_out": w_out, "w_cross_query": w_cross_query, "w_cross_kv": w_cross_kv, "w_cross_out": w_cross_out, "encoded": encoded, "owners": owners, "slots": slots}


norm_eps = 1e-05

def rms_scaled(inputs, gain_vector):
    floats = inputs.astype(jnp.float32)
    return floats * lax.rsqrt(lax.optimization_barrier(jnp.mean(floats * floats, axis=-1, keepdims=True)) + norm_eps) * gain_vector.astype(jnp.float32)

def split_sum(inputs, weight):
    group_width = inputs.shape[1] // N_MP

    def add_group(running, group_index):
        left_part = lax.dynamic_slice_in_dim(inputs, group_index * group_width, group_width, 1)
        right_part = lax.dynamic_slice_in_dim(weight, group_index * group_width, group_width, 0)
        partial_sum = jnp.dot(left_part, right_part, preferred_element_type=jnp.float32).astype(jnp.bfloat16)
        partial_sum = lax.optimization_barrier(partial_sum)
        return (running + partial_sum.astype(jnp.float32), None)
    start_sum = jnp.zeros((inputs.shape[0], weight.shape[1]), jnp.float32)
    summed, unused = lax.scan(add_group, start_sum, jnp.arange(N_MP, dtype=jnp.int32))
    return summed

def self_attend(queries, keys_all, values_all):
    score_scale = HEAD ** (-0.5)
    key_pos = jnp.arange(LEN, dtype=jnp.int32)

    def one_block(block_index):
        block_queries = lax.dynamic_slice_in_dim(queries, block_index * TOK_DEV, TOK_DEV, 0)
        scores = jnp.einsum('qhe,khe->hqk', block_queries.astype(jnp.float32), keys_all.astype(jnp.float32)) * score_scale
        query_pos = block_index * TOK_DEV + jnp.arange(TOK_DEV, dtype=jnp.int32)
        allowed = key_pos[None, :] <= query_pos[:, None]
        scores = jnp.where(allowed[None], scores, -jnp.inf)
        peak = lax.optimization_barrier(jnp.max(scores, axis=-1, keepdims=True))
        weights = jnp.exp(scores - peak)
        totals = lax.optimization_barrier(jnp.sum(weights, axis=-1))
        rounded = lax.optimization_barrier(weights.astype(jnp.bfloat16))
        mixed_out = jnp.einsum('hqk,khe->qhe', rounded.astype(jnp.float32), values_all.astype(jnp.float32))
        return (mixed_out / jnp.transpose(totals)[:, :, None]).astype(jnp.bfloat16)
    blocks = lax.map(one_block, jnp.arange(N_CTX, dtype=jnp.int32))
    return blocks.reshape(LEN, HEADS * HEAD)

def cross_attend(queries, keys_nb, values_nb):
    score_scale = HEAD ** (-0.5)
    lag_rows = SPAN - 1
    shifted = jnp.concatenate([queries[lag_rows:], jnp.zeros((lag_rows, HEADS, HEAD), jnp.bfloat16)], axis=0)
    shifted = shifted.reshape(SPANS, SPAN, HEADS, HEAD)
    keys_flat = keys_nb.reshape(SPANS, NB_PER * NB_TOK, HEADS, HEAD)
    values_flat = values_nb.reshape(SPANS, NB_PER * NB_TOK, HEADS, HEAD)
    scores = jnp.einsum('cmhe,cnhe->chmn', shifted.astype(jnp.float32), keys_flat.astype(jnp.float32)) * score_scale
    peak = lax.optimization_barrier(jnp.max(scores, axis=-1, keepdims=True))
    weights = jnp.exp(scores - peak)
    totals = lax.optimization_barrier(jnp.sum(weights, axis=-1))
    rounded = lax.optimization_barrier(weights.astype(jnp.bfloat16))
    mixed_out = jnp.einsum('chmn,cnhe->cmhe', rounded.astype(jnp.float32), values_flat.astype(jnp.float32))
    mixed_out = (mixed_out / jnp.transpose(totals, (0, 2, 1))[..., None]).astype(jnp.bfloat16)
    mixed_out = mixed_out.reshape(LEN, HEADS * HEAD)
    return jnp.concatenate([jnp.zeros((lag_rows, HEADS * HEAD), jnp.bfloat16), mixed_out[:LEN - lag_rows]], axis=0)

def reference(tokens, norm_gain, cross_gain, w_query, w_key, w_value, w_out, w_cross_query, w_cross_kv, w_cross_out, encoded, owners, slots):
    results = []
    for seq_index in range(SEQS):
        seq_tokens = tokens[seq_index]
        normed = rms_scaled(seq_tokens, norm_gain).astype(jnp.bfloat16)
        queries = jnp.dot(normed, w_query, preferred_element_type=jnp.float32).astype(jnp.bfloat16).reshape(LEN, HEADS, HEAD)
        keys_all = jnp.dot(normed, w_key, preferred_element_type=jnp.float32).astype(jnp.bfloat16).reshape(LEN, HEADS, HEAD)
        values_all = jnp.dot(normed, w_value, preferred_element_type=jnp.float32).astype(jnp.bfloat16).reshape(LEN, HEADS, HEAD)
        attended = self_attend(queries, keys_all, values_all)
        mixed = (seq_tokens.astype(jnp.float32) + split_sum(attended, w_out)).astype(jnp.bfloat16)
        cross_in = rms_scaled(mixed, cross_gain).astype(jnp.bfloat16)
        cross_queries = jnp.dot(cross_in, w_cross_query, preferred_element_type=jnp.float32).astype(jnp.bfloat16).reshape(LEN, HEADS, HEAD)
        row_ids = (owners[seq_index] * ENC_DEV + slots[seq_index]).reshape(-1).astype(jnp.int32)
        fetched = encoded[row_ids].astype(jnp.float32)
        keys_nb = jnp.einsum('nrw,wd->nrd', fetched, w_cross_kv[0].astype(jnp.float32)).astype(jnp.bfloat16)
        values_nb = jnp.einsum('nrw,wd->nrd', fetched, w_cross_kv[1].astype(jnp.float32)).astype(jnp.bfloat16)
        keys_nb = keys_nb.reshape(SPANS, NB_PER, NB_TOK, HEADS, HEAD)
        values_nb = values_nb.reshape(SPANS, NB_PER, NB_TOK, HEADS, HEAD)
        crossed = cross_attend(cross_queries, keys_nb, values_nb)
        results.append((mixed.astype(jnp.float32) + split_sum(crossed, w_cross_out)).astype(jnp.bfloat16))
    return jnp.stack(results)
```

```python
import jax
import jax.numpy as jnp
from jax import lax
from jax.experimental import pallas as pl
from jax.experimental.pallas import tpu as pltpu
from jax.sharding import PartitionSpec as P

HEAD = 128
SPAN = 64
NB_TOK = 128
NB_PER = 2
LOG2E = 1.4426950408889634
norm_eps = 1e-05
mask_floor = -1e30

CHIPS = ((0, 0), (0, -1), (0, 1), (1, 0), (0, 2), (1, -1), (1, 1), (1, 2))


def route(dy, dx, dc):
    return [
        (y * 8 + x * 2 + c, ((y + dy) % 2) * 8 + ((x + dx) % 4) * 2 + (c + dc) % 2)
        for y in range(2)
        for x in range(4)
        for c in range(2)
    ]


TO_RIGHT, TO_LEFT, TO_Y, TO_CORE = route(0, 1, 0), route(0, -1, 0), route(1, 0, 0), route(0, 0, 1)


def mp_send(block, pairs):
    return lax.ppermute(block, "mp", pairs)


def relative_ids():
    me = lax.axis_index("mp")
    y, x, c = me // 8, (me // 2) % 4, me % 2
    return jnp.stack(
        [
            ((y + dy) % 2) * 8 + ((x + dx) % 4) * 2 + (c + dc) % 2
            for dc in range(2)
            for dy, dx in CHIPS
        ]
    ).astype(jnp.int32)


def gather_mp(shard):
    half = shard.shape[0] // 2
    from_left, from_right, from_y = (
        mp_send(shard, TO_RIGHT),
        mp_send(shard, TO_LEFT),
        mp_send(shard, TO_Y),
    )
    left2 = mp_send(jnp.concatenate([from_left[:half], from_y[:half]]), TO_RIGHT)
    right2 = mp_send(jnp.concatenate([from_right[half:], from_y[half:]]), TO_LEFT)
    across = mp_send(jnp.concatenate([from_left[half:], from_right[:half]]), TO_Y)
    far_top = mp_send(left2[half:], TO_RIGHT)
    far_low = mp_send(right2[half:], TO_LEFT)
    mine = jnp.stack(
        [
            shard,
            from_left,
            from_right,
            from_y,
            jnp.concatenate([left2[:half], right2[:half]]),
            jnp.concatenate([left2[half:], across[:half]]),
            jnp.concatenate([across[half:], right2[half:]]),
            jnp.concatenate([far_top, far_low]),
        ]
    )
    return mine, mp_send(mine, TO_CORE)


def scatter_mp(mine, partner):
    partner = mp_send(partner, TO_CORE)

    def part(i, rows):
        return mine[i, rows].astype(jnp.float32) + partner[i, rows].astype(jnp.float32)

    half = mine.shape[1] // 2
    top, low = slice(0, half), slice(half, 2 * half)
    b16 = jnp.bfloat16
    own, left, right, y, x2, y_left, y_right, y2 = range(8)
    from_left = mp_send(jnp.concatenate([part(x2, top), part(y2, top)]).astype(b16), TO_RIGHT)
    from_right = mp_send(jnp.concatenate([part(x2, low), part(y2, low)]).astype(b16), TO_LEFT)
    from_y = mp_send(jnp.concatenate([part(y_right, low), part(y_left, top)]).astype(b16), TO_Y)
    via_left = mp_send((part(y_right, top) + from_left[half:].astype(jnp.float32)).astype(b16), TO_RIGHT)
    via_right = mp_send((part(y_left, low) + from_right[half:].astype(jnp.float32)).astype(b16), TO_LEFT)
    to_right = jnp.concatenate(
        [
            part(right, top) + from_left[:half].astype(jnp.float32),
            part(right, low) + from_y[:half].astype(jnp.float32),
        ]
    ).astype(b16)
    to_left = jnp.concatenate(
        [
            part(left, top) + from_y[half:].astype(jnp.float32),
            part(left, low) + from_right[:half].astype(jnp.float32),
        ]
    ).astype(b16)
    to_y = (
        part(y, slice(0, 2 * half))
        + jnp.concatenate([via_left, via_right]).astype(jnp.float32)
    ).astype(b16)
    a, b, c = mp_send(to_right, TO_RIGHT), mp_send(to_left, TO_LEFT), mp_send(to_y, TO_Y)
    return (
        part(own, slice(0, 2 * half))
        + a.astype(jnp.float32)
        + b.astype(jnp.float32)
        + c.astype(jnp.float32)
    )


VMEM_ROOM = 48 * 1024 * 1024


def call(kernel, **kw):
    return pl.pallas_call(
        kernel,
        compiler_params=pltpu.CompilerParams(vmem_limit_bytes=VMEM_ROOM),
        **kw,
    )


def normed_projection(ids, mine, partner, gain, weights):
    count = len(weights)
    shards, rows, feats = mine.shape
    steps = 2 * shards
    width = weights[0].shape[1]

    def kernel(ids_ref, mine_ref, partner_ref, gain_ref, *refs):
        w_refs, out_refs = refs[:count], refs[count : 2 * count]
        inv_ref, acc_ref = refs[2 * count :]
        k = pl.program_id(0)

        @pl.when(k == 0)
        def _():
            total = jnp.zeros((rows, feats), jnp.float32)
            for i in range(shards):
                a = mine_ref[i].astype(jnp.float32)
                b = partner_ref[i].astype(jnp.float32)
                total = total + a * a + b * b
            mean = jnp.sum(total, axis=1, keepdims=True) * (1.0 / (steps * feats))
            inv_ref[...] = jnp.broadcast_to(lax.rsqrt(mean + norm_eps), inv_ref.shape)

        def step(x):
            normed = (
                x.astype(jnp.float32) * inv_ref[:, :1] * gain_ref[ids_ref[k]]
            ).astype(jnp.bfloat16)
            for i in range(count):
                part = jnp.dot(normed, w_refs[i][...], preferred_element_type=jnp.float32)
                acc_ref[i] = jnp.where(k == 0, part, acc_ref[i] + part)

        @pl.when(k < shards)
        def _():
            step(mine_ref[jnp.minimum(k, shards - 1)])

        @pl.when(k >= shards)
        def _():
            step(partner_ref[jnp.maximum(k - shards, 0)])

        @pl.when(k == steps - 1)
        def _():
            for i in range(count):
                out_refs[i][...] = acc_ref[i].astype(jnp.bfloat16)

    whole = pl.BlockSpec((shards, rows, feats), lambda k, ids: (0, 0, 0))
    return call(
        kernel,
        grid_spec=pltpu.PrefetchScalarGridSpec(
            num_scalar_prefetch=1,
            grid=(steps,),
            in_specs=[
                whole,
                whole,
                pl.BlockSpec((steps, 1, feats), lambda k, ids: (0, 0, 0)),
            ]
            + [pl.BlockSpec((feats, width), lambda k, ids: (ids[k], 0))] * count,
            out_specs=[pl.BlockSpec((rows, width), lambda k, ids: (0, 0))] * count,
            scratch_shapes=[
                pltpu.VMEM((rows, 128), jnp.float32),
                pltpu.VMEM((count, rows, width), jnp.float32),
            ],
        ),
        out_shape=[jax.ShapeDtypeStruct((rows, width), jnp.bfloat16)] * count,
    )(ids, mine, partner, gain.reshape(steps, 1, feats), *weights)


def self_attention(queries, kv_own, kv_back1, kv_back2, kv_back3):
    rows, width = queries.shape
    heads = width // HEAD
    chunk = rows // 2
    scale = HEAD ** (-0.5) * LOG2E

    def kernel(ctx_ref, q_ref, own_ref, b1_ref, b2_ref, b3_ref, out_ref):
        c = pl.program_id(0)
        kv = (own_ref, b1_ref, b2_ref, b3_ref)
        for back in range(4):

            @pl.when(ctx_ref[0] == back)
            def _(back=back):
                pos = c * chunk + lax.broadcasted_iota(jnp.int32, (chunk, rows), 0)
                allowed = lax.broadcasted_iota(jnp.int32, (chunk, rows), 1) <= pos
                for h in range(heads):
                    cols = slice(h * HEAD, (h + 1) * HEAD)
                    q = q_ref[:, cols]
                    scores = []
                    for d in range(back + 1):
                        s = lax.dot_general(
                            q,
                            kv[d][0, :, cols],
                            (((1,), (1,)), ((), ())),
                            preferred_element_type=jnp.float32,
                        ) * scale
                        scores.append(jnp.where(allowed, s, mask_floor) if d == 0 else s)
                    peak = jnp.max(scores[0], axis=1, keepdims=True)
                    for s in scores[1:]:
                        peak = jnp.maximum(peak, jnp.max(s, axis=1, keepdims=True))
                    total, mixed = 0.0, 0.0
                    for d in range(back + 1):
                        weights = jnp.exp2(scores[d] - peak)
                        total = total + jnp.sum(weights, axis=1, keepdims=True)
                        mixed = mixed + jnp.dot(
                            weights.astype(jnp.bfloat16),
                            kv[d][1, :, cols],
                            preferred_element_type=jnp.float32,
                        )
                    out_ref[:, cols] = (mixed / total).astype(jnp.bfloat16)

    whole = pl.BlockSpec((2, rows, width), lambda c, ctx: (0, 0, 0))
    block = pl.BlockSpec((chunk, width), lambda c, ctx: (c, 0))
    return call(
        kernel,
        grid_spec=pltpu.PrefetchScalarGridSpec(
            num_scalar_prefetch=1, grid=(2,), in_specs=[block] + [whole] * 4, out_specs=block
        ),
        out_shape=jax.ShapeDtypeStruct((rows, width), jnp.bfloat16),
    )(lax.axis_index("ctx").reshape(1).astype(jnp.int32), queries, kv_own, kv_back1, kv_back2, kv_back3)


def output_blocks(ids, inputs, weight):
    rows, depth = inputs.shape
    blocks = ids.shape[0]
    width = 256

    def kernel(ids_ref, in_ref, w_ref, out_ref):
        out_ref[0] = jnp.dot(in_ref[...], w_ref[...], preferred_element_type=jnp.float32).astype(
            jnp.bfloat16
        )

    return call(
        kernel,
        grid_spec=pltpu.PrefetchScalarGridSpec(
            num_scalar_prefetch=1,
            grid=(blocks,),
            in_specs=[
                pl.BlockSpec((rows, depth), lambda k, ids: (0, 0)),
                pl.BlockSpec((depth, width), lambda k, ids: (0, ids[k])),
            ],
            out_specs=pl.BlockSpec((1, rows, width), lambda k, ids: (k, 0, 0)),
        ),
        out_shape=jax.ShapeDtypeStruct((blocks, rows, width), jnp.bfloat16),
    )(ids, inputs, weight)


def neighbour_projection(mine, partner, w_cross_kv):
    shards, rows, depth = mine.shape
    width = w_cross_kv.shape[2]
    spans = rows // 16

    def kernel(mine_ref, partner_ref, w_ref, out_ref):
        for core, x_ref in enumerate((mine_ref, partner_ref)):
            for part in range(2):
                res = jnp.dot(x_ref[0], w_ref[part], preferred_element_type=jnp.float32)
                out_ref[part, :, 0, core] = res.astype(jnp.bfloat16).reshape(spans, 16, width)

    block = pl.BlockSpec((1, rows, depth), lambda k: (k, 0, 0))
    return call(
        kernel,
        grid=(shards,),
        in_specs=[block, block, pl.BlockSpec((2, depth, width), lambda k: (0, 0, 0))],
        out_specs=pl.BlockSpec((2, spans, 1, 2, 16, width), lambda k: (0, 0, k, 0, 0, 0)),
        out_shape=jax.ShapeDtypeStruct((2, spans, shards, 2, 16, width), jnp.bfloat16),
    )(mine, partner, w_cross_kv).reshape(2, spans, shards * 32, width)


def cross_attention(queries, neighbour_kv, earlier):
    rows, width = queries.shape
    heads = width // HEAD
    spans = neighbour_kv.shape[1]
    scale = HEAD ** (-0.5) * LOG2E

    def attend(q, k, v):
        s = (
            lax.dot_general(q, k, (((1,), (1,)), ((), ())), preferred_element_type=jnp.float32)
            * scale
        )
        weights = jnp.exp2(s - jnp.max(s, axis=1, keepdims=True))
        total = jnp.sum(weights, axis=1, keepdims=True)
        return jnp.dot(weights.astype(jnp.bfloat16), v, preferred_element_type=jnp.float32) / total

    def kernel(q_ref, kv_ref, earlier_ref, out_ref, shifted_ref):
        row = lax.broadcasted_iota(jnp.int32, (rows, HEAD), 0)
        for h in range(heads):
            cols = slice(h * HEAD, (h + 1) * HEAD)
            shifted = pltpu.roll(q_ref[:, cols].astype(jnp.float32), 1, 0).astype(jnp.bfloat16)
            for g in range(spans):
                k, v = (
                    (earlier_ref[0, :, cols], earlier_ref[1, :, cols])
                    if g == 0
                    else (kv_ref[0, g - 1, :, cols], kv_ref[1, g - 1, :, cols])
                )
                shifted_ref[g * SPAN : (g + 1) * SPAN] = attend(
                    shifted[g * SPAN : (g + 1) * SPAN], k, v
                )
            last = attend(
                q_ref[rows - 16 :, cols], kv_ref[0, spans - 1, :, cols], kv_ref[1, spans - 1, :, cols]
            )
            back = pltpu.roll(shifted_ref[...], rows - 1, 0)
            final = jnp.where(row == rows - 1, last[15:16], back)
            out_ref[:, cols] = final.astype(jnp.bfloat16)

    return call(
        kernel,
        out_shape=jax.ShapeDtypeStruct((rows, width), jnp.bfloat16),
        scratch_shapes=[pltpu.VMEM((rows, HEAD), jnp.float32)],
    )(queries, neighbour_kv, earlier)


def fetch_neighbours(encoded, owners, slots):
    group_count = lax.axis_size(("pool", "ctx"))
    my_group = lax.axis_index(("pool", "ctx"))
    per_group = owners.size // group_count
    capacity = max(2, 2 * per_group // group_count)
    owner_table = owners.reshape(group_count, per_group)
    slot_table = slots.reshape(group_count, per_group)
    matched = (owner_table == my_group).astype(jnp.int32)
    earlier = jnp.arange(per_group)[None, :] < jnp.arange(per_group)[:, None]
    order_rank = jnp.sum(matched[:, None, :] * earlier.astype(jnp.int32)[None], axis=2)
    slot_index = jnp.arange(capacity, dtype=jnp.int32)
    picked = matched[:, None, :] * (order_rank[:, None, :] == slot_index[None, :, None]).astype(
        jnp.int32
    )
    source_rows = jnp.sum(picked * slot_table[:, None, :], axis=2).reshape(-1)
    outgoing = encoded[source_rows]
    outgoing = outgoing.reshape((group_count, capacity) + encoded.shape[1:])
    incoming = lax.all_to_all(outgoing, ("pool", "ctx"), split_axis=0, concat_axis=0, tiled=True)
    wanted = lax.dynamic_index_in_dim(owner_table, my_group, 0, keepdims=False)
    same_owner = (wanted[:, None] == wanted[None, :]).astype(jnp.int32)
    arrival = wanted * capacity + jnp.sum(same_owner * earlier.astype(jnp.int32), axis=1)
    return incoming.reshape((group_count * capacity,) + encoded.shape[1:])[arrival]


def ctx_send(block, pairs):
    return lax.ppermute(block, "ctx", pairs)


def relay_kv(kv):
    half = kv.shape[1] // 2
    back1 = ctx_send(kv, [(0, 1), (1, 2), (2, 3)])
    other = ctx_send(kv, [(0, 3), (1, 0)])
    top = ctx_send(back1[:, :half], [(1, 2), (2, 3)])
    low = ctx_send(other[:, half:], [(3, 2), (0, 3)])
    return back1, jnp.concatenate([top, low], axis=1), other


def per_device(
    tokens,
    norm_gain,
    cross_gain,
    w_query,
    w_key,
    w_value,
    w_out,
    w_cross_query,
    w_cross_kv,
    w_cross_out,
    encoded,
    owners,
    slots,
):
    ids = relative_ids()
    half = ids.shape[0] // 2
    mine, partner = gather_mp(tokens[0])
    fetched = fetch_neighbours(encoded, owners, slots)
    keys, values = normed_projection(ids, mine, partner, norm_gain, (w_key, w_value))
    kv = jnp.stack([keys, values])
    back1, back2, back3 = relay_kv(kv)
    (queries,) = normed_projection(ids, mine, partner, norm_gain, (w_query,))
    nb_mine, nb_partner = gather_mp(fetched.reshape(-1, fetched.shape[-1]))
    neighbour_kv = neighbour_projection(nb_mine, nb_partner, w_cross_kv)
    earlier = ctx_send(neighbour_kv[:, -1], [(0, 1), (1, 2), (2, 3)])
    attended = self_attention(queries, kv, back1, back2, back3)
    for_partner = output_blocks(ids[half:], attended, w_out)
    for_mine = output_blocks(ids[:half], attended, w_out)
    share = scatter_mp(for_mine, for_partner)
    residual = (tokens[0].astype(jnp.float32) + share).astype(jnp.bfloat16)
    mine, partner = gather_mp(residual)
    (cross_queries,) = normed_projection(ids, mine, partner, cross_gain, (w_cross_query,))
    crossed = cross_attention(cross_queries, neighbour_kv, earlier)
    for_partner = output_blocks(ids[half:], crossed, w_cross_out)
    for_mine = output_blocks(ids[:half], crossed, w_cross_out)
    share = scatter_mp(for_mine, for_partner)
    return (residual.astype(jnp.float32) + share).astype(jnp.bfloat16)[None]


def solution(mesh):
    placed = (
        P("pool", "ctx", "mp"),
        P(),
        P(),
        P(None, "mp"),
        P(None, "mp"),
        P(None, "mp"),
        P("mp", None),
        P(None, "mp"),
        P(None, None, "mp"),
        P("mp", None),
        P(("pool", "ctx"), "mp", None),
        P(),
        P(),
    )
    return jax.shard_map(
        per_device, mesh=mesh, in_specs=placed, out_specs=P("pool", "ctx", "mp"), check_vma=False
    )
```

```python
import jax
import jax.numpy as jnp
from jax import lax
from jax.experimental import pallas as pl
from jax.experimental.pallas import tpu as pltpu
from jax.sharding import PartitionSpec as P

HEAD = 128
SPAN = 64
NB_TOK = 128
NB_PER = 2
LOG2E = 1.4426950408889634
norm_eps = 1e-05
mask_floor = -1e30

CHIPS = ((0, 0), (0, -1), (0, 1), (1, 0), (0, 2), (1, -1), (1, 1), (1, 2))


def route(dy, dx, dc):
    return [
        (y * 8 + x * 2 + c, ((y + dy) % 2) * 8 + ((x + dx) % 4) * 2 + (c + dc) % 2)
        for y in range(2)
        for x in range(4)
        for c in range(2)
    ]


TO_RIGHT, TO_LEFT, TO_X2 = route(0, 1, 0), route(0, -1, 0), route(0, 2, 0)
TO_Y, TO_CORE = route(1, 0, 0), route(0, 0, 1)


def mp_send(block, pairs):
    return lax.ppermute(block, "mp", pairs)


def relative_ids():
    me = lax.axis_index("mp")
    y, x, c = me // 8, (me // 2) % 4, me % 2
    return jnp.stack(
        [
            ((y + dy) % 2) * 8 + ((x + dx) % 4) * 2 + (c + dc) % 2
            for dc in range(2)
            for dy, dx in CHIPS
        ]
    ).astype(jnp.int32)


def corner(block):
    return block[(0,) * (block.ndim - 2) + (slice(0, 16), slice(0, 128))]


def gather_mp(shard, during_first=None, during_second=None, all_first=False):
    tie = lax.optimization_barrier
    from_y, from_x2 = mp_send(shard, TO_Y), mp_send(shard, TO_X2)
    from_left, from_right = mp_send(shard, TO_RIGHT), mp_send(shard, TO_LEFT)
    if all_first:
        (from_y, from_x2, from_left, from_right), during_first = tie(
            ((from_y, from_x2, from_left, from_right), during_first)
        )
    else:
        (from_y, from_x2), during_first = tie(((from_y, from_x2), during_first))
    left_y, right_y = mp_send(from_y, TO_RIGHT), mp_send(from_y, TO_LEFT)
    y_x2 = mp_send(from_x2, TO_Y)
    near = jnp.stack([shard, from_left, from_right, from_y])
    near_partner = mp_send(near, TO_CORE)
    if callable(during_second):
        during_second = during_second(during_first)
    far, during_second, _ = tie(
        (jnp.stack([from_x2, left_y, right_y, y_x2]), during_second, corner(near))
    )
    return (near, far, near_partner, mp_send(far, TO_CORE)), during_first, during_second


def scatter_mp(mine, partner, during_first=None):
    partner = mp_send(partner, TO_CORE)

    def part(i):
        return mine[i].astype(jnp.float32) + partner[i].astype(jnp.float32)

    b16, f32 = jnp.bfloat16, jnp.float32
    _, left, right, y, x2, y_left, y_right, y2 = range(8)
    far = mp_send(part(y2).astype(b16), TO_Y)
    from_left = mp_send(part(y_right).astype(b16), TO_RIGHT)
    from_right = mp_send(part(y_left).astype(b16), TO_LEFT)
    near_left = mp_send(part(right).astype(b16), TO_RIGHT)
    near_right = mp_send(part(left).astype(b16), TO_LEFT)
    (far, from_left, from_right), during_first = lax.optimization_barrier(
        ((far, from_left, from_right), during_first)
    )
    from_x2 = mp_send((part(x2) + far.astype(f32)).astype(b16), TO_X2)
    from_y = mp_send((part(y) + from_left.astype(f32) + from_right.astype(f32)).astype(b16), TO_Y)
    return [mine, partner, near_left, near_right, from_x2, from_y], during_first


IN_VMEM = pl.BlockSpec(memory_space=pltpu.VMEM)
MIB = 1024 * 1024


def call(kernel, room, **kw):
    return pl.pallas_call(
        kernel,
        compiler_params=pltpu.CompilerParams(vmem_limit_bytes=room * MIB),
        **kw,
    )


STAT_ROWS = 16


def shard_to_send(ids, gain, summands):
    rows, feats = summands[0].shape[-2:]
    pick = [s.ndim == 3 for s in summands]

    def kernel(ids_ref, gain_ref, *refs):
        in_refs, (plain_ref, out_ref) = refs[:-2], refs[-2:]
        total = jnp.zeros((rows, feats), jnp.float32)
        for ref, leading in zip(in_refs, pick):
            total = total + (ref[0] if leading else ref[...]).astype(jnp.float32)
        plain = total.astype(jnp.bfloat16)
        plain_ref[...] = plain
        x = plain.astype(jnp.float32)
        out_ref[:rows] = (x * gain_ref[ids_ref[0]]).astype(jnp.bfloat16)
        squares = jnp.broadcast_to(jnp.sum(x * x, axis=1, keepdims=True), (rows, 128)).T
        line = jnp.concatenate(
            [squares[:1, i * feats : (i + 1) * feats] for i in range(rows // feats)]
        )
        high = line.astype(jnp.bfloat16).astype(jnp.float32)
        block = jnp.concatenate(
            [high, line - high, jnp.zeros((STAT_ROWS - 2 * (rows // feats), feats), jnp.float32)]
        )
        out_ref[rows:] = block.astype(jnp.bfloat16)

    return call(
        kernel,
        8,
        in_specs=[pl.BlockSpec(memory_space=pltpu.SMEM)] + [IN_VMEM] * (1 + len(summands)),
        out_specs=[IN_VMEM] * 2,
        out_shape=[
            jax.ShapeDtypeStruct((rows, feats), jnp.bfloat16),
            jax.ShapeDtypeStruct((rows + STAT_ROWS, feats), jnp.bfloat16),
        ],
    )(ids[:1], gain.reshape(-1, 1, feats), *summands)


def normed_projection(ids, stacks, weights):
    each, rows, feats = stacks[0].shape
    rows = rows - STAT_ROWS
    depth = each * len(stacks) * feats
    count = len(weights)
    width = weights[0].shape[1]
    lines = rows // feats

    def kernel(ids_ref, *refs):
        x_refs, w_refs = refs[: len(stacks)], refs[len(stacks) : -1]
        out_ref = refs[-1]
        stat = jnp.zeros((STAT_ROWS, feats), jnp.float32)
        for x_ref in x_refs:
            for i in range(each):
                stat = stat + x_ref[i, rows:].astype(jnp.float32)
        stat = stat[:lines] + stat[lines : 2 * lines]
        inv_line = lax.rsqrt(stat * (1.0 / depth) + norm_eps)
        inv = jnp.concatenate(
            [jnp.broadcast_to(inv_line[i : i + 1], (128, feats)).T for i in range(lines)]
        )
        inv = jnp.concatenate([inv] * (width // 128), axis=1)
        x = jnp.concatenate([x_ref[i, :rows] for x_ref in x_refs for i in range(each)], axis=1)
        for i, w_ref in enumerate(w_refs):
            w = jnp.concatenate(
                [
                    w_ref[pl.ds(pl.multiple_of(ids_ref[k] * feats, feats), feats)]
                    for k in range(each * len(stacks))
                ]
            )
            product = jnp.dot(x, w, preferred_element_type=jnp.float32)
            out_ref[i] = (product * inv).astype(jnp.bfloat16)

    return call(
        kernel,
        12,
        in_specs=[pl.BlockSpec(memory_space=pltpu.SMEM)] + [IN_VMEM] * (len(stacks) + count),
        out_specs=IN_VMEM,
        out_shape=jax.ShapeDtypeStruct((count, rows, width), jnp.bfloat16),
        cost_estimate=pl.CostEstimate(
            flops=2 * rows * depth * width * count,
            bytes_accessed=2 * (rows + width * count) * depth,
            transcendentals=0,
        ),
    )(ids, *stacks, *weights)


def self_attention(queries, kv_own, kv_back1, kv_back2, kv_back3):
    rows, width = queries.shape
    heads = width // HEAD
    chunk = rows // 2
    scale = HEAD ** (-0.5) * LOG2E

    def kernel(ctx_ref, q_ref, own_ref, b1_ref, b2_ref, b3_ref, out_ref):
        kv = (own_ref, b1_ref, b2_ref, b3_ref)
        start = pl.program_id(0) * chunk
        for back in range(4):

            @pl.when(ctx_ref[0] == back)
            def _(back=back):
                pos = start + lax.broadcasted_iota(jnp.int32, (chunk, rows), 0)
                allowed = lax.broadcasted_iota(jnp.int32, (chunk, rows), 1) <= pos
                for h in range(heads):
                    cols = slice(h * HEAD, (h + 1) * HEAD)
                    q = q_ref[:, cols]
                    scores = []
                    for d in range(back + 1):
                        s = lax.dot_general(
                            q,
                            kv[d][0, :, cols],
                            (((1,), (1,)), ((), ())),
                            preferred_element_type=jnp.float32,
                        ) * scale
                        scores.append(jnp.where(allowed, s, mask_floor) if d == 0 else s)
                    peak = jnp.max(scores[0], axis=1, keepdims=True)
                    for s in scores[1:]:
                        peak = jnp.maximum(peak, jnp.max(s, axis=1, keepdims=True))
                    total, mixed = 0.0, 0.0
                    for d in range(back + 1):
                        weights = jnp.exp2(scores[d] - peak)
                        total = total + jnp.sum(weights, axis=1, keepdims=True)
                        mixed = mixed + jnp.dot(
                            weights.astype(jnp.bfloat16),
                            kv[d][1, :, cols],
                            preferred_element_type=jnp.float32,
                        )
                    out_ref[:, cols] = (mixed / total).astype(jnp.bfloat16)

    whole = pl.BlockSpec((2, rows, width), lambda c: (0, 0, 0))
    block = pl.BlockSpec((chunk, width), lambda c: (c, 0))
    return call(
        kernel,
        16,
        grid=(rows // chunk,),
        in_specs=[pl.BlockSpec(memory_space=pltpu.SMEM), block] + [whole] * 4,
        out_specs=block,
        out_shape=jax.ShapeDtypeStruct((rows, width), jnp.bfloat16),
        cost_estimate=pl.CostEstimate(
            flops=16 * rows * rows * width,
            bytes_accessed=10 * rows * width,
            transcendentals=8 * rows * rows,
        ),
    )(lax.axis_index("ctx").reshape(1).astype(jnp.int32), queries, kv_own, kv_back1, kv_back2, kv_back3)


def output_blocks(ids, inputs, weight):
    rows = inputs.shape[0]
    blocks = ids.shape[0]
    width = 256

    def kernel(ids_ref, in_ref, w_ref, out_ref):
        for k in range(blocks):
            start = pl.multiple_of(ids_ref[k] * width, width)
            out_ref[k] = jnp.dot(
                in_ref[...], w_ref[:, pl.ds(start, width)], preferred_element_type=jnp.float32
            ).astype(jnp.bfloat16)

    return call(
        kernel,
        12,
        in_specs=[pl.BlockSpec(memory_space=pltpu.SMEM), IN_VMEM, IN_VMEM],
        out_specs=IN_VMEM,
        out_shape=jax.ShapeDtypeStruct((blocks, rows, width), jnp.bfloat16),
        cost_estimate=pl.CostEstimate(
            flops=2 * rows * inputs.shape[1] * width * blocks,
            bytes_accessed=2 * rows * width * blocks,
            transcendentals=0,
        ),
    )(ids, inputs, weight)


def neighbour_projection(stacks, w_cross_kv):
    each, rows, depth = stacks[0].shape
    width = w_cross_kv.shape[2]
    spans = rows // 16

    def kernel(*refs):
        x_refs, w_ref, out_ref = refs[:-2], refs[-2], refs[-1]
        for n, x_ref in enumerate(x_refs):
            x = x_ref[...].reshape(each * rows, depth)
            for part in range(2):
                res = jnp.dot(x, w_ref[part], preferred_element_type=jnp.float32)
                res = res.astype(jnp.bfloat16).reshape(each, spans, 16, width)
                for i in range(each):
                    out_ref[part, :, n * each + i] = res[i]

    return call(
        kernel,
        16,
        in_specs=[IN_VMEM] * (len(stacks) + 1),
        out_specs=IN_VMEM,
        out_shape=jax.ShapeDtypeStruct((2, spans, each * len(stacks), 16, width), jnp.bfloat16),
        cost_estimate=pl.CostEstimate(
            flops=4 * rows * each * len(stacks) * depth * width,
            bytes_accessed=2 * rows * each * len(stacks) * depth,
            transcendentals=0,
        ),
    )(*stacks, w_cross_kv)


def cross_attention(queries, neighbour_kv, earlier):
    rows, width = queries.shape
    heads = width // HEAD
    spans = neighbour_kv.shape[1]
    tokens = NB_PER * NB_TOK
    scale = HEAD ** (-0.5) * LOG2E

    def kernel(q_ref, kv_ref, earlier_ref, out_ref):
        row = lax.broadcasted_iota(jnp.int32, (rows, HEAD), 0)

        def span(part, g, cols):
            ref = earlier_ref.at[part] if g == 0 else kv_ref.at[part, g - 1]
            return ref[:, :, cols].reshape(tokens, HEAD)

        for h in range(heads):
            cols = slice(h * HEAD, (h + 1) * HEAD)
            q = q_ref[:, cols]
            shifted = pltpu.roll(q.astype(jnp.float32), 1, 0).astype(jnp.bfloat16)
            groups = [shifted[g * SPAN : (g + 1) * SPAN] for g in range(spans)] + [q[rows - 16 :]]
            s = jnp.concatenate(
                [
                    lax.dot_general(
                        groups[g],
                        span(0, g, cols),
                        (((1,), (1,)), ((), ())),
                        preferred_element_type=jnp.float32,
                    )
                    for g in range(spans + 1)
                ]
            )
            s = s * scale
            weights = jnp.exp2(s - jnp.max(s, axis=1, keepdims=True))
            total = jnp.sum(weights, axis=1, keepdims=True)
            weights = weights.astype(jnp.bfloat16)
            mixed = jnp.concatenate(
                [
                    jnp.dot(
                        weights[g * SPAN : min((g + 1) * SPAN, rows + 16)],
                        span(1, g, cols),
                        preferred_element_type=jnp.float32,
                    )
                    for g in range(spans + 1)
                ]
            )
            mixed = mixed / total
            back = pltpu.roll(mixed[:rows], rows - 1, 0)
            final = jnp.where(row == rows - 1, mixed[rows + 15 :], back)
            out_ref[:, cols] = final.astype(jnp.bfloat16)

    return call(
        kernel,
        12,
        in_specs=[IN_VMEM] * 3,
        out_specs=IN_VMEM,
        out_shape=jax.ShapeDtypeStruct((rows, width), jnp.bfloat16),
    )(queries, neighbour_kv, earlier)


def pick_neighbours(encoded, owners, slots):
    group_count = lax.axis_size(("pool", "ctx"))
    my_group = lax.axis_index(("pool", "ctx"))
    per_group = owners.size // group_count
    capacity = max(2, 2 * per_group // group_count)
    owner_table = owners.reshape(group_count, per_group)
    slot_table = slots.reshape(group_count, per_group)
    matched = (owner_table == my_group).astype(jnp.int32)
    earlier = jnp.arange(per_group)[None, :] < jnp.arange(per_group)[:, None]
    order_rank = jnp.sum(matched[:, None, :] * earlier.astype(jnp.int32)[None], axis=2)
    slot_index = jnp.arange(capacity, dtype=jnp.int32)
    picked = matched[:, None, :] * (order_rank[:, None, :] == slot_index[None, :, None]).astype(
        jnp.int32
    )
    source_rows = jnp.sum(picked * slot_table[:, None, :], axis=2).reshape(-1)
    outgoing = encoded[source_rows]
    outgoing = outgoing.reshape((group_count, capacity) + encoded.shape[1:])
    wanted = lax.dynamic_index_in_dim(owner_table, my_group, 0, keepdims=False)
    same_owner = (wanted[:, None] == wanted[None, :]).astype(jnp.int32)
    arrival = wanted * capacity + jnp.sum(same_owner * earlier.astype(jnp.int32), axis=1)
    return outgoing, arrival


def exchange_neighbours(outgoing, arrival):
    incoming = lax.all_to_all(outgoing, ("pool", "ctx"), split_axis=0, concat_axis=0, tiled=True)
    return incoming.reshape((-1,) + outgoing.shape[2:])[arrival]


def ctx_send(block, pairs):
    return lax.ppermute(block, "ctx", pairs)


def send_kv(kv):
    return ctx_send(kv, [(0, 1), (1, 2), (2, 3)]), ctx_send(kv, [(0, 3), (1, 0)])


def per_device(
    tokens,
    norm_gain,
    cross_gain,
    w_query,
    w_key,
    w_value,
    w_out,
    w_cross_query,
    w_cross_kv,
    w_cross_out,
    encoded,
    owners,
    slots,
):
    ids = relative_ids()
    half = ids.shape[0] // 2
    tie = lax.optimization_barrier
    _, shard = shard_to_send(ids, norm_gain, [tokens[0]])
    picked = pick_neighbours(encoded, owners, slots)
    fetched = exchange_neighbours(*picked)
    stacks, _, fetched = gather_mp(shard, picked, fetched)
    kv = normed_projection(ids, stacks, (w_key, w_value))
    kv, fetched = tie((kv, fetched))
    back1, back3 = send_kv(kv)
    queries = normed_projection(ids, stacks, (w_query,))[0]
    nb_stacks, _, attended = gather_mp(
        fetched.reshape(-1, fetched.shape[-1]),
        (corner(queries), corner(back3), corner(back1)),
        lambda _: self_attention(
            queries, kv, back1, ctx_send(back3, [(3, 2), (0, 3)]), back3
        ),
        all_first=True,
    )
    for_partner = output_blocks(ids[half:], attended, w_out)
    for_mine = output_blocks(ids[:half], attended, w_out)
    neighbour_kv = neighbour_projection(nb_stacks, w_cross_kv)
    summands, neighbour_kv = scatter_mp(for_mine, for_partner, neighbour_kv)
    earlier = ctx_send(neighbour_kv[:, -1], [(0, 1), (1, 2), (2, 3)])
    residual, shard = shard_to_send(ids, cross_gain, [tokens[0]] + summands)
    stacks, earlier, _ = gather_mp(shard, earlier)
    cross_queries = normed_projection(ids, stacks, (w_cross_query,))[0]
    crossed = cross_attention(cross_queries, neighbour_kv, earlier)
    for_partner = output_blocks(ids[half:], crossed, w_cross_out)
    for_mine = output_blocks(ids[:half], crossed, w_cross_out)
    summands, _ = scatter_mp(for_mine, for_partner)
    total = residual.astype(jnp.float32)
    for s in summands:
        total = total + (s[0] if s.ndim == 3 else s).astype(jnp.float32)
    return total.astype(jnp.bfloat16)[None]


def solution(mesh):
    placed = (
        P("pool", "ctx", "mp"),
        P(),
        P(),
        P(None, "mp"),
        P(None, "mp"),
        P(None, "mp"),
        P("mp", None),
        P(None, "mp"),
        P(None, None, "mp"),
        P("mp", None),
        P(("pool", "ctx"), "mp", None),
        P(),
        P(),
    )
    return jax.shard_map(
        per_device, mesh=mesh, in_specs=placed, out_specs=P("pool", "ctx", "mp"), check_vma=False
    )
```

```python
import jax
import jax.numpy as jnp
from jax import lax
from jax.experimental import pallas as pl
from jax.experimental.pallas import tpu as pltpu
from jax.sharding import PartitionSpec as P

HEAD = 128
SPAN = 64
NB_TOK = 128
NB_PER = 2
LOG2E = 1.4426950408889634
norm_eps = 1e-05
mask_floor = -1e30

CHIPS = ((0, 0), (0, -1), (0, 1), (0, 2), (1, 0), (1, -1), (1, 1), (1, 2))


def route(dy, dx, dc):
    return [
        (y * 8 + x * 2 + c, ((y + dy) % 2) * 8 + ((x + dx) % 4) * 2 + (c + dc) % 2)
        for y in range(2)
        for x in range(4)
        for c in range(2)
    ]


TO_RIGHT, TO_LEFT, TO_X2 = route(0, 1, 0), route(0, -1, 0), route(0, 2, 0)
TO_Y, TO_CORE = route(1, 0, 0), route(0, 0, 1)


def mp_send(block, pairs):
    return lax.ppermute(block, "mp", pairs)


def relative_ids():
    me = lax.axis_index("mp")
    y, x, c = me // 8, (me // 2) % 4, me % 2
    return jnp.stack(
        [
            ((y + dy) % 2) * 8 + ((x + dx) % 4) * 2 + (c + dc) % 2
            for dc in range(2)
            for dy, dx in CHIPS
        ]
    ).astype(jnp.int32)


def corner(block):
    return block[(0,) * (block.ndim - 2) + (slice(0, 16), slice(0, 128))]


def gather_mp(shard, during_first=None, during_second=None, all_first=False):
    tie = lax.optimization_barrier
    from_y, from_x2 = mp_send(shard, TO_Y), mp_send(shard, TO_X2)
    from_left, from_right = mp_send(shard, TO_RIGHT), mp_send(shard, TO_LEFT)
    if all_first:
        (from_y, from_x2, from_left, from_right), during_first = tie(
            ((from_y, from_x2, from_left, from_right), during_first)
        )
    else:
        (from_y, from_x2), during_first = tie(((from_y, from_x2), during_first))
    left_y, right_y = mp_send(from_y, TO_RIGHT), mp_send(from_y, TO_LEFT)
    y_x2 = mp_send(from_x2, TO_Y)
    near = jnp.stack([shard, from_left, from_right, from_x2])
    near_partner = mp_send(near, TO_CORE)
    if callable(during_second):
        during_second = during_second(during_first)
    far, during_second, _ = tie(
        (jnp.stack([from_y, left_y, right_y, y_x2]), during_second, corner(near))
    )
    return (near, far, near_partner, mp_send(far, TO_CORE)), during_first, during_second


def scatter_mp(mine, partner, during_first=None):
    partner = mp_send(partner, TO_CORE)

    def part(i):
        return mine[i].astype(jnp.float32) + partner[i].astype(jnp.float32)

    b16, f32 = jnp.bfloat16, jnp.float32
    _, left, right, x2, y, y_left, y_right, y2 = range(8)
    far = mp_send(part(y2).astype(b16), TO_Y)
    from_left = mp_send(part(y_right).astype(b16), TO_RIGHT)
    from_right = mp_send(part(y_left).astype(b16), TO_LEFT)
    near_left = mp_send(part(right).astype(b16), TO_RIGHT)
    near_right = mp_send(part(left).astype(b16), TO_LEFT)
    (far, from_left, from_right), during_first = lax.optimization_barrier(
        ((far, from_left, from_right), during_first)
    )
    from_x2 = mp_send((part(x2) + far.astype(f32)).astype(b16), TO_X2)
    from_y = mp_send((part(y) + from_left.astype(f32) + from_right.astype(f32)).astype(b16), TO_Y)
    return [mine, partner, near_left, near_right, from_x2, from_y], during_first


IN_VMEM = pl.BlockSpec(memory_space=pltpu.VMEM)
MIB = 1024 * 1024


def call(kernel, room, **kw):
    return pl.pallas_call(
        kernel,
        compiler_params=pltpu.CompilerParams(vmem_limit_bytes=room * MIB),
        **kw,
    )


STAT_ROWS = 16


def shard_to_send(ids, gain, summands):
    rows, feats = summands[0].shape[-2:]
    pick = [s.ndim == 3 for s in summands]

    def kernel(ids_ref, gain_ref, *refs):
        in_refs, (plain_ref, out_ref) = refs[:-2], refs[-2:]
        total = jnp.zeros((rows, feats), jnp.float32)
        for ref, leading in zip(in_refs, pick):
            total = total + (ref[0] if leading else ref[...]).astype(jnp.float32)
        plain = total.astype(jnp.bfloat16)
        plain_ref[...] = plain
        x = plain.astype(jnp.float32)
        out_ref[:rows] = (x * gain_ref[ids_ref[0]]).astype(jnp.bfloat16)
        squares = jnp.broadcast_to(jnp.sum(x * x, axis=1, keepdims=True), (rows, 128)).T
        line = jnp.concatenate(
            [squares[:1, i * feats : (i + 1) * feats] for i in range(rows // feats)]
        )
        high = line.astype(jnp.bfloat16).astype(jnp.float32)
        block = jnp.concatenate(
            [high, line - high, jnp.zeros((STAT_ROWS - 2 * (rows // feats), feats), jnp.float32)]
        )
        out_ref[rows:] = block.astype(jnp.bfloat16)

    return call(
        kernel,
        8,
        in_specs=[pl.BlockSpec(memory_space=pltpu.SMEM)] + [IN_VMEM] * (1 + len(summands)),
        out_specs=[IN_VMEM] * 2,
        out_shape=[
            jax.ShapeDtypeStruct((rows, feats), jnp.bfloat16),
            jax.ShapeDtypeStruct((rows + STAT_ROWS, feats), jnp.bfloat16),
        ],
    )(ids[:1], gain.reshape(-1, 1, feats), *summands)


def normed_projection(ids, stacks, weights):
    each, rows, feats = stacks[0].shape
    rows = rows - STAT_ROWS
    depth = each * len(stacks) * feats
    count = len(weights)
    width = weights[0].shape[1]
    lines = rows // feats

    def kernel(ids_ref, *refs):
        x_refs, w_refs = refs[: len(stacks)], refs[len(stacks) : -1]
        out_ref = refs[-1]
        stat = jnp.zeros((STAT_ROWS, feats), jnp.float32)
        for x_ref in x_refs:
            for i in range(each):
                stat = stat + x_ref[i, rows:].astype(jnp.float32)
        stat = stat[:lines] + stat[lines : 2 * lines]
        inv_line = lax.rsqrt(stat * (1.0 / depth) + norm_eps)
        inv = jnp.concatenate(
            [jnp.broadcast_to(inv_line[i : i + 1], (128, feats)).T for i in range(lines)]
        )
        inv = jnp.concatenate([inv] * (width // 128), axis=1)
        x = jnp.concatenate([x_ref[i, :rows] for x_ref in x_refs for i in range(each)], axis=1)
        for i, w_ref in enumerate(w_refs):
            w = jnp.concatenate(
                [
                    w_ref[pl.ds(pl.multiple_of(ids_ref[k] * feats, feats), feats)]
                    for k in range(each * len(stacks))
                ]
            )
            product = jnp.dot(x, w, preferred_element_type=jnp.float32)
            out_ref[i] = (product * inv).astype(jnp.bfloat16)

    return call(
        kernel,
        12,
        in_specs=[pl.BlockSpec(memory_space=pltpu.SMEM)] + [IN_VMEM] * (len(stacks) + count),
        out_specs=IN_VMEM,
        out_shape=jax.ShapeDtypeStruct((count, rows, width), jnp.bfloat16),
        cost_estimate=pl.CostEstimate(
            flops=2 * rows * depth * width * count,
            bytes_accessed=2 * (rows + width * count) * depth,
            transcendentals=0,
        ),
    )(ids, *stacks, *weights)


def halved_projection(ids, stacks, weights):
    near, far, near_partner, far_partner = stacks
    each, rows, feats = near.shape
    rows = rows - STAT_ROWS
    depth = 4 * each * feats
    count = len(weights)
    width = weights[0].shape[1]
    lines = rows // feats

    def kernel(ids_ref, near_ref, far_ref, near_partner_ref, far_partner_ref, *refs):
        w_refs, out_ref, acc_ref = refs[:count], refs[count], refs[count + 1]
        step = pl.program_id(0)

        def product(first, second, at, w_ref):
            x = jnp.concatenate([r[i, :rows] for r in (first, second) for i in range(each)], axis=1)
            w = jnp.concatenate(
                [
                    w_ref[pl.ds(pl.multiple_of((ids_ref[k] % (2 * each)) * feats, feats), feats)]
                    for part in (at, at + 2 * each)
                    for k in range(part, part + each)
                ]
            )
            return jnp.dot(x, w, preferred_element_type=jnp.float32)

        @pl.when(step == 0)
        def _():
            for i, w_ref in enumerate(w_refs):
                acc_ref[i] = product(near_ref, near_partner_ref, 0, w_ref)

        @pl.when(step == 1)
        def _():
            stat = jnp.zeros((STAT_ROWS, feats), jnp.float32)
            for x_ref in (near_ref, far_ref, near_partner_ref, far_partner_ref):
                for i in range(each):
                    stat = stat + x_ref[i, rows:].astype(jnp.float32)
            stat = stat[:lines] + stat[lines : 2 * lines]
            inv_line = lax.rsqrt(stat * (1.0 / depth) + norm_eps)
            inv = jnp.concatenate(
                [jnp.broadcast_to(inv_line[i : i + 1], (128, feats)).T for i in range(lines)]
            )
            inv = jnp.concatenate([inv] * (width // 128), axis=1)
            for i, w_ref in enumerate(w_refs):
                total = acc_ref[i] + product(far_ref, far_partner_ref, each, w_ref)
                out_ref[i] = (total * inv).astype(jnp.bfloat16)

    whole = pl.BlockSpec(near.shape, lambda g, ids: (0, 0, 0))
    return call(
        kernel,
        48,
        grid_spec=pltpu.PrefetchScalarGridSpec(
            num_scalar_prefetch=1,
            grid=(2,),
            in_specs=[whole] * 4
            + [
                pl.BlockSpec(
                    (2 * each * feats, width), lambda g, ids: ((ids[0] // (2 * each) + g) % 2, 0)
                )
            ]
            * count,
            out_specs=pl.BlockSpec((count, rows, width), lambda g, ids: (0, 0, 0)),
            scratch_shapes=[pltpu.VMEM((count, rows, width), jnp.float32)],
        ),
        out_shape=jax.ShapeDtypeStruct((count, rows, width), jnp.bfloat16),
        cost_estimate=pl.CostEstimate(
            flops=2 * rows * depth * width * count,
            bytes_accessed=2 * (rows + width * count) * depth,
            transcendentals=0,
        ),
    )(ids, *stacks, *weights)


def self_attention(queries, kv_own, kv_back1, kv_back2, kv_back3):
    rows, width = queries.shape
    heads = width // HEAD
    chunk = rows // 2
    scale = HEAD ** (-0.5) * LOG2E

    def kernel(ctx_ref, q_ref, own_ref, b1_ref, b2_ref, b3_ref, out_ref):
        kv = (own_ref, b1_ref, b2_ref, b3_ref)
        start = pl.program_id(0) * chunk
        for back in range(4):

            @pl.when(ctx_ref[0] == back)
            def _(back=back):
                pos = start + lax.broadcasted_iota(jnp.int32, (chunk, rows), 0)
                allowed = lax.broadcasted_iota(jnp.int32, (chunk, rows), 1) <= pos
                for h in range(heads):
                    cols = slice(h * HEAD, (h + 1) * HEAD)
                    q = q_ref[:, cols]
                    scores = []
                    for d in range(back + 1):
                        s = lax.dot_general(
                            q,
                            kv[d][0, :, cols],
                            (((1,), (1,)), ((), ())),
                            preferred_element_type=jnp.float32,
                        ) * scale
                        scores.append(jnp.where(allowed, s, mask_floor) if d == 0 else s)
                    peak = jnp.max(scores[0], axis=1, keepdims=True)
                    for s in scores[1:]:
                        peak = jnp.maximum(peak, jnp.max(s, axis=1, keepdims=True))
                    total, mixed = 0.0, 0.0
                    for d in range(back + 1):
                        weights = jnp.exp2(scores[d] - peak)
                        total = total + jnp.sum(weights, axis=1, keepdims=True)
                        mixed = mixed + jnp.dot(
                            weights.astype(jnp.bfloat16),
                            kv[d][1, :, cols],
                            preferred_element_type=jnp.float32,
                        )
                    out_ref[:, cols] = (mixed / total).astype(jnp.bfloat16)

    whole = pl.BlockSpec((2, rows, width), lambda c: (0, 0, 0))
    block = pl.BlockSpec((chunk, width), lambda c: (c, 0))
    return call(
        kernel,
        16,
        grid=(rows // chunk,),
        in_specs=[pl.BlockSpec(memory_space=pltpu.SMEM), block] + [whole] * 4,
        out_specs=block,
        out_shape=jax.ShapeDtypeStruct((rows, width), jnp.bfloat16),
        cost_estimate=pl.CostEstimate(
            flops=16 * rows * rows * width,
            bytes_accessed=10 * rows * width,
            transcendentals=8 * rows * rows,
        ),
    )(lax.axis_index("ctx").reshape(1).astype(jnp.int32), queries, kv_own, kv_back1, kv_back2, kv_back3)


def output_blocks(ids, inputs, weight):
    rows = inputs.shape[0]
    blocks = ids.shape[0]
    width = 256

    def kernel(ids_ref, in_ref, w_ref, out_ref):
        for k in range(blocks):
            start = pl.multiple_of(ids_ref[k] * width, width)
            out_ref[k] = jnp.dot(
                in_ref[...], w_ref[:, pl.ds(start, width)], preferred_element_type=jnp.float32
            ).astype(jnp.bfloat16)

    return call(
        kernel,
        12,
        in_specs=[pl.BlockSpec(memory_space=pltpu.SMEM), IN_VMEM, IN_VMEM],
        out_specs=IN_VMEM,
        out_shape=jax.ShapeDtypeStruct((blocks, rows, width), jnp.bfloat16),
        cost_estimate=pl.CostEstimate(
            flops=2 * rows * inputs.shape[1] * width * blocks,
            bytes_accessed=2 * rows * width * blocks,
            transcendentals=0,
        ),
    )(ids, inputs, weight)


def neighbour_projection(stacks, w_cross_kv):
    each, rows, depth = stacks[0].shape
    width = w_cross_kv.shape[2]
    spans = rows // 16

    def kernel(*refs):
        x_refs, w_ref, out_ref = refs[:-2], refs[-2], refs[-1]
        for n, x_ref in enumerate(x_refs):
            x = x_ref[...].reshape(each * rows, depth)
            for part in range(2):
                res = jnp.dot(x, w_ref[part], preferred_element_type=jnp.float32)
                res = res.astype(jnp.bfloat16).reshape(each, spans, 16, width)
                for i in range(each):
                    out_ref[part, :, n * each + i] = res[i]

    return call(
        kernel,
        16,
        in_specs=[IN_VMEM] * (len(stacks) + 1),
        out_specs=IN_VMEM,
        out_shape=jax.ShapeDtypeStruct((2, spans, each * len(stacks), 16, width), jnp.bfloat16),
        cost_estimate=pl.CostEstimate(
            flops=4 * rows * each * len(stacks) * depth * width,
            bytes_accessed=2 * rows * each * len(stacks) * depth,
            transcendentals=0,
        ),
    )(*stacks, w_cross_kv)


def cross_attention(queries, neighbour_kv, earlier):
    rows, width = queries.shape
    heads = width // HEAD
    spans = neighbour_kv.shape[1]
    tokens = NB_PER * NB_TOK
    scale = HEAD ** (-0.5) * LOG2E

    def kernel(q_ref, kv_ref, earlier_ref, out_ref):
        row = lax.broadcasted_iota(jnp.int32, (rows, HEAD), 0)

        def span(part, g, cols):
            ref = earlier_ref.at[part] if g == 0 else kv_ref.at[part, g - 1]
            return ref[:, :, cols].reshape(tokens, HEAD)

        for h in range(heads):
            cols = slice(h * HEAD, (h + 1) * HEAD)
            q = q_ref[:, cols]
            shifted = pltpu.roll(q.astype(jnp.float32), 1, 0).astype(jnp.bfloat16)
            groups = [shifted[g * SPAN : (g + 1) * SPAN] for g in range(spans)] + [q[rows - 16 :]]
            s = jnp.concatenate(
                [
                    lax.dot_general(
                        groups[g],
                        span(0, g, cols),
                        (((1,), (1,)), ((), ())),
                        preferred_element_type=jnp.float32,
                    )
                    for g in range(spans + 1)
                ]
            )
            s = s * scale
            weights = jnp.exp2(s - jnp.max(s, axis=1, keepdims=True))
            total = jnp.sum(weights, axis=1, keepdims=True)
            weights = weights.astype(jnp.bfloat16)
            mixed = jnp.concatenate(
                [
                    jnp.dot(
                        weights[g * SPAN : min((g + 1) * SPAN, rows + 16)],
                        span(1, g, cols),
                        preferred_element_type=jnp.float32,
                    )
                    for g in range(spans + 1)
                ]
            )
            mixed = mixed / total
            back = pltpu.roll(mixed[:rows], rows - 1, 0)
            final = jnp.where(row == rows - 1, mixed[rows + 15 :], back)
            out_ref[:, cols] = final.astype(jnp.bfloat16)

    return call(
        kernel,
        12,
        in_specs=[IN_VMEM] * 3,
        out_specs=IN_VMEM,
        out_shape=jax.ShapeDtypeStruct((rows, width), jnp.bfloat16),
    )(queries, neighbour_kv, earlier)


def pick_neighbours(encoded, owners, slots):
    group_count = lax.axis_size(("pool", "ctx"))
    my_group = lax.axis_index(("pool", "ctx"))
    per_group = owners.size // group_count
    capacity = max(2, 2 * per_group // group_count)
    owner_table = owners.reshape(group_count, per_group)
    slot_table = slots.reshape(group_count, per_group)
    matched = (owner_table == my_group).astype(jnp.int32)
    earlier = jnp.arange(per_group)[None, :] < jnp.arange(per_group)[:, None]
    order_rank = jnp.sum(matched[:, None, :] * earlier.astype(jnp.int32)[None], axis=2)
    slot_index = jnp.arange(capacity, dtype=jnp.int32)
    picked = matched[:, None, :] * (order_rank[:, None, :] == slot_index[None, :, None]).astype(
        jnp.int32
    )
    source_rows = jnp.sum(picked * slot_table[:, None, :], axis=2).reshape(-1)
    outgoing = encoded[source_rows]
    outgoing = outgoing.reshape((group_count, capacity) + encoded.shape[1:])
    wanted = lax.dynamic_index_in_dim(owner_table, my_group, 0, keepdims=False)
    same_owner = (wanted[:, None] == wanted[None, :]).astype(jnp.int32)
    arrival = wanted * capacity + jnp.sum(same_owner * earlier.astype(jnp.int32), axis=1)
    return outgoing, arrival


def exchange_neighbours(outgoing, arrival):
    incoming = lax.all_to_all(outgoing, ("pool", "ctx"), split_axis=0, concat_axis=0, tiled=True)
    return incoming.reshape((-1,) + outgoing.shape[2:])[arrival]


def ctx_send(block, pairs):
    return lax.ppermute(block, "ctx", pairs)


def send_kv(kv):
    return ctx_send(kv, [(0, 1), (1, 2), (2, 3)]), ctx_send(kv, [(0, 3), (1, 0)])


def per_device(
    tokens,
    norm_gain,
    cross_gain,
    w_query,
    w_key,
    w_value,
    w_out,
    w_cross_query,
    w_cross_kv,
    w_cross_out,
    encoded,
    owners,
    slots,
):
    ids = relative_ids()
    half = ids.shape[0] // 2
    tie = lax.optimization_barrier
    _, shard = shard_to_send(ids, norm_gain, [tokens[0]])
    picked = pick_neighbours(encoded, owners, slots)
    fetched = exchange_neighbours(*picked)
    stacks, _, fetched = gather_mp(shard, picked, fetched)
    kv = halved_projection(ids, stacks, (w_key, w_value))
    kv, fetched = tie((kv, fetched))
    back1, back3 = send_kv(kv)
    queries = normed_projection(ids, stacks, (w_query,))[0]
    nb_stacks, _, attended = gather_mp(
        fetched.reshape(-1, fetched.shape[-1]),
        (corner(queries), corner(back3), corner(back1)),
        lambda _: self_attention(
            queries, kv, back1, ctx_send(back3, [(3, 2), (0, 3)]), back3
        ),
        all_first=True,
    )
    for_partner = output_blocks(ids[half:], attended, w_out)
    for_mine = output_blocks(ids[:half], attended, w_out)
    neighbour_kv = neighbour_projection(nb_stacks, w_cross_kv)
    summands, neighbour_kv = scatter_mp(for_mine, for_partner, neighbour_kv)
    earlier = ctx_send(neighbour_kv[:, -1], [(0, 1), (1, 2), (2, 3)])
    residual, shard = shard_to_send(ids, cross_gain, [tokens[0]] + summands)
    stacks, earlier, _ = gather_mp(shard, earlier)
    cross_queries = normed_projection(ids, stacks, (w_cross_query,))[0]
    crossed = cross_attention(cross_queries, neighbour_kv, earlier)
    for_partner = output_blocks(ids[half:], crossed, w_cross_out)
    for_mine = output_blocks(ids[:half], crossed, w_cross_out)
    summands, _ = scatter_mp(for_mine, for_partner)
    total = residual.astype(jnp.float32)
    for s in summands:
        total = total + (s[0] if s.ndim == 3 else s).astype(jnp.float32)
    return total.astype(jnp.bfloat16)[None]


def solution(mesh):
    placed = (
        P("pool", "ctx", "mp"),
        P(),
        P(),
        P(None, "mp"),
        P(None, "mp"),
        P(None, "mp"),
        P("mp", None),
        P(None, "mp"),
        P(None, None, "mp"),
        P("mp", None),
        P(("pool", "ctx"), "mp", None),
        P(),
        P(),
    )
    return jax.shard_map(
        per_device, mesh=mesh, in_specs=placed, out_specs=P("pool", "ctx", "mp"), check_vma=False
    )
```

```python
import jax
import jax.numpy as jnp
from jax import lax
from jax.experimental import pallas as pl
from jax.experimental.pallas import tpu as pltpu
from jax.sharding import PartitionSpec as P

HEAD = 128
SPAN = 64
NB_TOK = 128
NB_PER = 2
LOG2E = 1.4426950408889634
norm_eps = 1e-05
mask_floor = -1e30

CHIPS = ((0, 0), (0, -1), (0, 1), (0, 2), (1, 0), (1, -1), (1, 1), (1, 2))


def route(dy, dx, dc):
    return [
        (y * 8 + x * 2 + c, ((y + dy) % 2) * 8 + ((x + dx) % 4) * 2 + (c + dc) % 2)
        for y in range(2)
        for x in range(4)
        for c in range(2)
    ]


TO_RIGHT, TO_LEFT, TO_X2 = route(0, 1, 0), route(0, -1, 0), route(0, 2, 0)
TO_Y, TO_CORE = route(1, 0, 0), route(0, 0, 1)


def mp_send(block, pairs):
    return lax.ppermute(block, "mp", pairs)


def relative_ids():
    me = lax.axis_index("mp")
    y, x, c = me // 8, (me // 2) % 4, me % 2
    return jnp.stack(
        [
            ((y + dy) % 2) * 8 + ((x + dx) % 4) * 2 + (c + dc) % 2
            for dc in range(2)
            for dy, dx in CHIPS
        ]
    ).astype(jnp.int32)


def corner(block):
    return block[(0,) * (block.ndim - 2) + (slice(0, 16), slice(0, 128))]


def gather_mp(shard, during_first=None, during_second=None, all_first=False):
    tie = lax.optimization_barrier
    from_y, from_x2 = mp_send(shard, TO_Y), mp_send(shard, TO_X2)
    from_left, from_right = mp_send(shard, TO_RIGHT), mp_send(shard, TO_LEFT)
    if all_first:
        (from_y, from_x2, from_left, from_right), during_first = tie(
            ((from_y, from_x2, from_left, from_right), during_first)
        )
    else:
        (from_y, from_x2), during_first = tie(((from_y, from_x2), during_first))
    left_y, right_y = mp_send(from_y, TO_RIGHT), mp_send(from_y, TO_LEFT)
    y_x2 = mp_send(from_x2, TO_Y)
    near = jnp.stack([shard, from_left, from_right, from_x2])
    near_partner = mp_send(near, TO_CORE)
    if callable(during_second):
        during_second = during_second(during_first)
    far, during_second, _ = tie(
        (jnp.stack([from_y, left_y, right_y, y_x2]), during_second, corner(near))
    )
    return (near, far, near_partner, mp_send(far, TO_CORE)), during_first, during_second


def scatter_mp(mine, partner, during_first=None):
    near, far = mp_send(partner[0], TO_CORE), mp_send(partner[1], TO_CORE)
    count = near.shape[0]

    def part(i):
        other = near[i] if i < count else far[i - count]
        return mine[i].astype(jnp.float32) + other.astype(jnp.float32)

    b16, f32 = jnp.bfloat16, jnp.float32
    _, left, right, x2, y, y_left, y_right, y2 = range(8)
    via_y = mp_send(part(y2).astype(b16), TO_Y)
    from_left = mp_send(part(y_right).astype(b16), TO_RIGHT)
    from_right = mp_send(part(y_left).astype(b16), TO_LEFT)
    near_left = mp_send(part(right).astype(b16), TO_RIGHT)
    near_right = mp_send(part(left).astype(b16), TO_LEFT)
    (via_y, from_left, from_right), during_first = lax.optimization_barrier(
        ((via_y, from_left, from_right), during_first)
    )
    from_x2 = mp_send((part(x2) + via_y.astype(f32)).astype(b16), TO_X2)
    from_y = mp_send((part(y) + from_left.astype(f32) + from_right.astype(f32)).astype(b16), TO_Y)
    return [mine, near, near_left, near_right, from_x2, from_y], during_first


IN_VMEM = pl.BlockSpec(memory_space=pltpu.VMEM)
MIB = 1024 * 1024


def call(kernel, room, **kw):
    return pl.pallas_call(
        kernel,
        compiler_params=pltpu.CompilerParams(vmem_limit_bytes=room * MIB),
        **kw,
    )


STAT_ROWS = 16


def shard_to_send(ids, gain, summands):
    rows, feats = summands[0].shape[-2:]
    pick = [s.ndim == 3 for s in summands]

    def kernel(ids_ref, gain_ref, *refs):
        in_refs, (plain_ref, out_ref) = refs[:-2], refs[-2:]
        total = jnp.zeros((rows, feats), jnp.float32)
        for ref, leading in zip(in_refs, pick):
            total = total + (ref[0] if leading else ref[...]).astype(jnp.float32)
        plain = total.astype(jnp.bfloat16)
        plain_ref[...] = plain
        x = plain.astype(jnp.float32)
        out_ref[:rows] = (x * gain_ref[ids_ref[0]]).astype(jnp.bfloat16)
        squares = jnp.broadcast_to(jnp.sum(x * x, axis=1, keepdims=True), (rows, 128)).T
        line = jnp.concatenate(
            [squares[:1, i * feats : (i + 1) * feats] for i in range(rows // feats)]
        )
        high = line.astype(jnp.bfloat16).astype(jnp.float32)
        block = jnp.concatenate(
            [high, line - high, jnp.zeros((STAT_ROWS - 2 * (rows // feats), feats), jnp.float32)]
        )
        out_ref[rows:] = block.astype(jnp.bfloat16)

    return call(
        kernel,
        8,
        in_specs=[pl.BlockSpec(memory_space=pltpu.SMEM)] + [IN_VMEM] * (1 + len(summands)),
        out_specs=[IN_VMEM] * 2,
        out_shape=[
            jax.ShapeDtypeStruct((rows, feats), jnp.bfloat16),
            jax.ShapeDtypeStruct((rows + STAT_ROWS, feats), jnp.bfloat16),
        ],
    )(ids[:1], gain.reshape(-1, 1, feats), *summands)


def normed_projection(ids, stacks, weights):
    each, rows, feats = stacks[0].shape
    rows = rows - STAT_ROWS
    depth = each * len(stacks) * feats
    count = len(weights)
    width = weights[0].shape[1]
    lines = rows // feats

    def kernel(ids_ref, *refs):
        x_refs, w_refs = refs[: len(stacks)], refs[len(stacks) : -1]
        out_ref = refs[-1]
        stat = jnp.zeros((STAT_ROWS, feats), jnp.float32)
        for x_ref in x_refs:
            for i in range(each):
                stat = stat + x_ref[i, rows:].astype(jnp.float32)
        stat = stat[:lines] + stat[lines : 2 * lines]
        inv_line = lax.rsqrt(stat * (1.0 / depth) + norm_eps)
        inv = jnp.concatenate(
            [jnp.broadcast_to(inv_line[i : i + 1], (128, feats)).T for i in range(lines)]
        )
        inv = jnp.concatenate([inv] * (width // 128), axis=1)
        x = jnp.concatenate([x_ref[i, :rows] for x_ref in x_refs for i in range(each)], axis=1)
        for i, w_ref in enumerate(w_refs):
            w = jnp.concatenate(
                [
                    w_ref[pl.ds(pl.multiple_of(ids_ref[k] * feats, feats), feats)]
                    for k in range(each * len(stacks))
                ]
            )
            product = jnp.dot(x, w, preferred_element_type=jnp.float32)
            out_ref[i] = (product * inv).astype(jnp.bfloat16)

    return call(
        kernel,
        12,
        in_specs=[pl.BlockSpec(memory_space=pltpu.SMEM)] + [IN_VMEM] * (len(stacks) + count),
        out_specs=IN_VMEM,
        out_shape=jax.ShapeDtypeStruct((count, rows, width), jnp.bfloat16),
        cost_estimate=pl.CostEstimate(
            flops=2 * rows * depth * width * count,
            bytes_accessed=2 * (rows + width * count) * depth,
            transcendentals=0,
        ),
    )(ids, *stacks, *weights)


def halved_projection(ids, stacks, weights):
    near, far, near_partner, far_partner = stacks
    each, rows, feats = near.shape
    rows = rows - STAT_ROWS
    depth = 4 * each * feats
    count = len(weights)
    width = weights[0].shape[1]
    lines = rows // feats

    def kernel(ids_ref, near_ref, far_ref, near_partner_ref, far_partner_ref, *refs):
        w_refs, out_ref, acc_ref = refs[:count], refs[count], refs[count + 1]
        step = pl.program_id(0)

        def product(first, second, at, w_ref):
            x = jnp.concatenate([r[i, :rows] for r in (first, second) for i in range(each)], axis=1)
            w = jnp.concatenate(
                [
                    w_ref[pl.ds(pl.multiple_of((ids_ref[k] % (2 * each)) * feats, feats), feats)]
                    for part in (at, at + 2 * each)
                    for k in range(part, part + each)
                ]
            )
            return jnp.dot(x, w, preferred_element_type=jnp.float32)

        @pl.when(step == 0)
        def _():
            for i, w_ref in enumerate(w_refs):
                acc_ref[i] = product(near_ref, near_partner_ref, 0, w_ref)

        @pl.when(step == 1)
        def _():
            stat = jnp.zeros((STAT_ROWS, feats), jnp.float32)
            for x_ref in (near_ref, far_ref, near_partner_ref, far_partner_ref):
                for i in range(each):
                    stat = stat + x_ref[i, rows:].astype(jnp.float32)
            stat = stat[:lines] + stat[lines : 2 * lines]
            inv_line = lax.rsqrt(stat * (1.0 / depth) + norm_eps)
            inv = jnp.concatenate(
                [jnp.broadcast_to(inv_line[i : i + 1], (128, feats)).T for i in range(lines)]
            )
            inv = jnp.concatenate([inv] * (width // 128), axis=1)
            for i, w_ref in enumerate(w_refs):
                total = acc_ref[i] + product(far_ref, far_partner_ref, each, w_ref)
                out_ref[i] = (total * inv).astype(jnp.bfloat16)

    whole = pl.BlockSpec(near.shape, lambda g, ids: (0, 0, 0))
    return call(
        kernel,
        48,
        grid_spec=pltpu.PrefetchScalarGridSpec(
            num_scalar_prefetch=1,
            grid=(2,),
            in_specs=[whole] * 4
            + [
                pl.BlockSpec(
                    (2 * each * feats, width), lambda g, ids: ((ids[0] // (2 * each) + g) % 2, 0)
                )
            ]
            * count,
            out_specs=pl.BlockSpec((count, rows, width), lambda g, ids: (0, 0, 0)),
            scratch_shapes=[pltpu.VMEM((count, rows, width), jnp.float32)],
        ),
        out_shape=jax.ShapeDtypeStruct((count, rows, width), jnp.bfloat16),
        cost_estimate=pl.CostEstimate(
            flops=2 * rows * depth * width * count,
            bytes_accessed=2 * (rows + width * count) * depth,
            transcendentals=0,
        ),
    )(ids, *stacks, *weights)


def self_attention(queries, kv_own, kv_back1, kv_back2, kv_back3):
    rows, width = queries.shape
    heads = width // HEAD
    chunk = rows // 2
    scale = HEAD ** (-0.5) * LOG2E

    def kernel(ctx_ref, q_ref, own_ref, b1_ref, b2_ref, b3_ref, out_ref):
        kv = (own_ref, b1_ref, b2_ref, b3_ref)
        start = pl.program_id(0) * chunk
        for back in range(4):

            @pl.when(ctx_ref[0] == back)
            def _(back=back):
                pos = start + lax.broadcasted_iota(jnp.int32, (chunk, rows), 0)
                allowed = lax.broadcasted_iota(jnp.int32, (chunk, rows), 1) <= pos
                for h in range(heads):
                    cols = slice(h * HEAD, (h + 1) * HEAD)
                    q = q_ref[:, cols]
                    scores = []
                    for d in range(back + 1):
                        s = lax.dot_general(
                            q,
                            kv[d][0, :, cols],
                            (((1,), (1,)), ((), ())),
                            preferred_element_type=jnp.float32,
                        ) * scale
                        scores.append(jnp.where(allowed, s, mask_floor) if d == 0 else s)
                    peak = jnp.max(scores[0], axis=1, keepdims=True)
                    for s in scores[1:]:
                        peak = jnp.maximum(peak, jnp.max(s, axis=1, keepdims=True))
                    total, mixed = 0.0, 0.0
                    for d in range(back + 1):
                        weights = jnp.exp2(scores[d] - peak)
                        total = total + jnp.sum(weights, axis=1, keepdims=True)
                        mixed = mixed + jnp.dot(
                            weights.astype(jnp.bfloat16),
                            kv[d][1, :, cols],
                            preferred_element_type=jnp.float32,
                        )
                    out_ref[:, cols] = (mixed / total).astype(jnp.bfloat16)

    whole = pl.BlockSpec((2, rows, width), lambda c: (0, 0, 0))
    block = pl.BlockSpec((chunk, width), lambda c: (c, 0))
    return call(
        kernel,
        16,
        grid=(rows // chunk,),
        in_specs=[pl.BlockSpec(memory_space=pltpu.SMEM), block] + [whole] * 4,
        out_specs=block,
        out_shape=jax.ShapeDtypeStruct((rows, width), jnp.bfloat16),
        cost_estimate=pl.CostEstimate(
            flops=16 * rows * rows * width,
            bytes_accessed=10 * rows * width,
            transcendentals=8 * rows * rows,
        ),
    )(lax.axis_index("ctx").reshape(1).astype(jnp.int32), queries, kv_own, kv_back1, kv_back2, kv_back3)


def output_blocks(ids, inputs, weight):
    rows = inputs.shape[0]
    blocks = ids.shape[0]
    width = 256

    def kernel(ids_ref, in_ref, w_ref, out_ref):
        for k in range(blocks):
            start = pl.multiple_of(ids_ref[k] * width, width)
            out_ref[k] = jnp.dot(
                in_ref[...], w_ref[:, pl.ds(start, width)], preferred_element_type=jnp.float32
            ).astype(jnp.bfloat16)

    return call(
        kernel,
        12,
        in_specs=[pl.BlockSpec(memory_space=pltpu.SMEM), IN_VMEM, IN_VMEM],
        out_specs=IN_VMEM,
        out_shape=jax.ShapeDtypeStruct((blocks, rows, width), jnp.bfloat16),
        cost_estimate=pl.CostEstimate(
            flops=2 * rows * inputs.shape[1] * width * blocks,
            bytes_accessed=2 * rows * width * blocks,
            transcendentals=0,
        ),
    )(ids, inputs, weight)


def neighbour_projection(stacks, w_cross_kv):
    each, rows, depth = stacks[0].shape
    width = w_cross_kv.shape[2]
    spans = rows // 16

    def kernel(*refs):
        x_refs, w_ref, out_ref = refs[:-2], refs[-2], refs[-1]
        for n, x_ref in enumerate(x_refs):
            x = x_ref[...].reshape(each * rows, depth)
            for part in range(2):
                res = jnp.dot(x, w_ref[part], preferred_element_type=jnp.float32)
                res = res.astype(jnp.bfloat16).reshape(each, spans, 16, width)
                for i in range(each):
                    out_ref[part, :, n * each + i] = res[i]

    return call(
        kernel,
        16,
        in_specs=[IN_VMEM] * (len(stacks) + 1),
        out_specs=IN_VMEM,
        out_shape=jax.ShapeDtypeStruct((2, spans, each * len(stacks), 16, width), jnp.bfloat16),
        cost_estimate=pl.CostEstimate(
            flops=4 * rows * each * len(stacks) * depth * width,
            bytes_accessed=2 * rows * each * len(stacks) * depth,
            transcendentals=0,
        ),
    )(*stacks, w_cross_kv)


def cross_attention(queries, neighbour_kv, earlier):
    rows, width = queries.shape
    heads = width // HEAD
    spans = neighbour_kv.shape[1]
    tokens = NB_PER * NB_TOK
    scale = HEAD ** (-0.5) * LOG2E

    def kernel(q_ref, kv_ref, earlier_ref, out_ref):
        row = lax.broadcasted_iota(jnp.int32, (rows, HEAD), 0)

        def span(part, g, cols):
            ref = earlier_ref.at[part] if g == 0 else kv_ref.at[part, g - 1]
            return ref[:, :, cols].reshape(tokens, HEAD)

        for h in range(heads):
            cols = slice(h * HEAD, (h + 1) * HEAD)
            q = q_ref[:, cols]
            shifted = pltpu.roll(q.astype(jnp.float32), 1, 0).astype(jnp.bfloat16)
            groups = [shifted[g * SPAN : (g + 1) * SPAN] for g in range(spans)] + [q[rows - 16 :]]
            s = jnp.concatenate(
                [
                    lax.dot_general(
                        groups[g],
                        span(0, g, cols),
                        (((1,), (1,)), ((), ())),
                        preferred_element_type=jnp.float32,
                    )
                    for g in range(spans + 1)
                ]
            )
            s = s * scale
            weights = jnp.exp2(s - jnp.max(s, axis=1, keepdims=True))
            total = jnp.sum(weights, axis=1, keepdims=True)
            weights = weights.astype(jnp.bfloat16)
            mixed = jnp.concatenate(
                [
                    jnp.dot(
                        weights[g * SPAN : min((g + 1) * SPAN, rows + 16)],
                        span(1, g, cols),
                        preferred_element_type=jnp.float32,
                    )
                    for g in range(spans + 1)
                ]
            )
            mixed = mixed / total
            back = pltpu.roll(mixed[:rows], rows - 1, 0)
            final = jnp.where(row == rows - 1, mixed[rows + 15 :], back)
            out_ref[:, cols] = final.astype(jnp.bfloat16)

    return call(
        kernel,
        12,
        in_specs=[IN_VMEM] * 3,
        out_specs=IN_VMEM,
        out_shape=jax.ShapeDtypeStruct((rows, width), jnp.bfloat16),
    )(queries, neighbour_kv, earlier)


def pick_neighbours(encoded, owners, slots):
    group_count = lax.axis_size(("pool", "ctx"))
    my_group = lax.axis_index(("pool", "ctx"))
    per_group = owners.size // group_count
    capacity = max(2, 2 * per_group // group_count)
    owner_table = owners.reshape(group_count, per_group)
    slot_table = slots.reshape(group_count, per_group)
    matched = (owner_table == my_group).astype(jnp.int32)
    earlier = jnp.arange(per_group)[None, :] < jnp.arange(per_group)[:, None]
    order_rank = jnp.sum(matched[:, None, :] * earlier.astype(jnp.int32)[None], axis=2)
    slot_index = jnp.arange(capacity, dtype=jnp.int32)
    picked = matched[:, None, :] * (order_rank[:, None, :] == slot_index[None, :, None]).astype(
        jnp.int32
    )
    source_rows = jnp.sum(picked * slot_table[:, None, :], axis=2).reshape(-1)
    outgoing = encoded[source_rows]
    outgoing = outgoing.reshape((group_count, capacity) + encoded.shape[1:])
    wanted = lax.dynamic_index_in_dim(owner_table, my_group, 0, keepdims=False)
    same_owner = (wanted[:, None] == wanted[None, :]).astype(jnp.int32)
    arrival = wanted * capacity + jnp.sum(same_owner * earlier.astype(jnp.int32), axis=1)
    return outgoing, arrival


def exchange_neighbours(outgoing, arrival):
    incoming = lax.all_to_all(outgoing, ("pool", "ctx"), split_axis=0, concat_axis=0, tiled=True)
    return incoming.reshape((-1,) + outgoing.shape[2:])[arrival]


def ctx_send(block, pairs):
    return lax.ppermute(block, "ctx", pairs)


def send_kv(kv):
    return ctx_send(kv, [(0, 1), (1, 2), (2, 3)]), ctx_send(kv, [(0, 3), (1, 0)])


def per_device(
    tokens,
    norm_gain,
    cross_gain,
    w_query,
    w_key,
    w_value,
    w_out,
    w_cross_query,
    w_cross_kv,
    w_cross_out,
    encoded,
    owners,
    slots,
):
    ids = relative_ids()
    half = ids.shape[0] // 2
    tie = lax.optimization_barrier
    _, shard = shard_to_send(ids, norm_gain, [tokens[0]])
    picked = pick_neighbours(encoded, owners, slots)
    fetched = exchange_neighbours(*picked)
    stacks, _, fetched = gather_mp(shard, picked, fetched)
    kv = halved_projection(ids, stacks, (w_key, w_value))
    kv, fetched = tie((kv, fetched))
    back1, back3 = send_kv(kv)
    queries = normed_projection(ids, stacks, (w_query,))[0]
    nb_stacks, _, attended = gather_mp(
        fetched.reshape(-1, fetched.shape[-1]),
        (corner(queries), corner(back3), corner(back1)),
        lambda _: self_attention(
            queries, kv, back1, ctx_send(back3, [(3, 2), (0, 3)]), back3
        ),
        all_first=True,
    )
    far_partner = output_blocks(ids[half + half // 2 :], attended, w_out)
    near_partner = output_blocks(ids[half : half + half // 2], attended, w_out)
    for_partner = (near_partner, far_partner)
    for_mine = output_blocks(ids[:half], attended, w_out)
    neighbour_kv = neighbour_projection(nb_stacks, w_cross_kv)
    summands, neighbour_kv = scatter_mp(for_mine, for_partner, neighbour_kv)
    earlier = ctx_send(neighbour_kv[:, -1], [(0, 1), (1, 2), (2, 3)])
    residual, shard = shard_to_send(ids, cross_gain, [tokens[0]] + summands)
    stacks, earlier, _ = gather_mp(shard, earlier)
    cross_queries = normed_projection(ids, stacks, (w_cross_query,))[0]
    crossed = cross_attention(cross_queries, neighbour_kv, earlier)
    far_partner = output_blocks(ids[half + half // 2 :], crossed, w_cross_out)
    near_partner = output_blocks(ids[half : half + half // 2], crossed, w_cross_out)
    for_partner = (near_partner, far_partner)
    for_mine = output_blocks(ids[:half], crossed, w_cross_out)
    summands, _ = scatter_mp(for_mine, for_partner)
    total = residual.astype(jnp.float32)
    for s in summands:
        total = total + (s[0] if s.ndim == 3 else s).astype(jnp.float32)
    return total.astype(jnp.bfloat16)[None]


def solution(mesh):
    placed = (
        P("pool", "ctx", "mp"),
        P(),
        P(),
        P(None, "mp"),
        P(None, "mp"),
        P(None, "mp"),
        P("mp", None),
        P(None, "mp"),
        P(None, None, "mp"),
        P("mp", None),
        P(("pool", "ctx"), "mp", None),
        P(),
        P(),
    )
    return jax.shard_map(
        per_device, mesh=mesh, in_specs=placed, out_specs=P("pool", "ctx", "mp"), check_vma=False
    )
```
